32 devices in a mesh: cluster: 8 (over z, x), camera: 4 (over y, core).
Axes of the slice: x: 2, y: 2, z: 4, core: 2. Of those that a mesh axis runs over, the one named last changes fastest.
Arguments:
- counts: int32 [8], replicated, may hold values from 1 to 16, as said below
- tiles: int32 [128, 4], replicated, may hold values from 0 to 3
- cam_jac: float32 [128, 128, 512], P('cluster', None, 'camera'), may hold values from -0.6 to 0.6
- point_jac: float32 [128, 128, 3, 512], P('cluster', None, None, 'camera'), may hold values from -0.15625 to 0.15625
- point_inv: float32 [128, 3, 3, 512], P('cluster', None, None, 'camera'), may hold values from -1 to 1, as said below
Outputs:
- reduced: float32 [4, 512, 2048], P('camera', 'cluster')
The draws below stay inside these ranges and needn't reach their ends.
Inputs may be any that keep to these rules, and one draw needn't show every extreme that they name: For every device i below 4, exactly one of the devices i and i + 4 holds 13 to 16 live clusters and the other 1 to 8; at least 4 devices hold exactly 16. The live clusters of a device are its first counts slots. Every 3x3 block point_inv[c, :, :, p] is symmetric and positive definite.
All inputs are finite; a program needn't handle non-finite values.
Results may differ from the reference program's by a relative error of at most 0.0003.
Values sent between devices are 32-bit elements; how exact they have to be, the bound alone decides.
A program may use at most 64 MiB of HBM per device.

```python
import jax
import jax.numpy as jnp
from jax import lax

CAMC = 512
PTS = 512
CAMS = 2048
ROWS = 128
KEEP = 12
EXTRA = 4
SLOTS = 16
CL_DEVICES = 8
CAM_DEVICES = 4
CLUSTERS = 128
GT = 4


def draw_counts(key, part):
    half_count = CL_DEVICES // 2
    pair_order = jax.random.permutation(jax.random.fold_in(key, 11), half_count)
    pair_rank = jnp.argsort(pair_order, stable=True)
    upper_heavy = jax.random.randint(jax.random.fold_in(key, 12), (half_count,), 0, 2)
    surplus = jax.random.randint(jax.random.fold_in(key, 13), (half_count,), 1, EXTRA + 1)
    surplus = jnp.where(pair_rank < EXTRA, EXTRA, surplus)
    heavy_count = KEEP + surplus
    light_count = jax.random.randint(jax.random.fold_in(key, 14), (half_count,), 1, KEEP - EXTRA + 1)
    light_count = jnp.where(pair_rank == 0, 1, light_count)
    lower_half = jnp.where(upper_heavy == 0, heavy_count, light_count)
    upper_half = jnp.where(upper_heavy == 1, heavy_count, light_count)
    return jnp.concatenate([lower_half, upper_half]).astype(jnp.int32)


def draw_point_inv(key, part):
    shape = (CLUSTERS, 3, PTS)
    exponent = jax.random.uniform(jax.random.fold_in(key, 21), shape, jnp.float32, jnp.log(0.25), 0.0)
    diagonal_part = jnp.exp(exponent)
    magnitude = jax.random.uniform(jax.random.fold_in(key, 22), shape, jnp.float32, 0.2, 0.45)
    sign_flip = jnp.where(jax.random.bernoulli(jax.random.fold_in(key, 23), 0.5, shape), 1.0, -1.0)
    coupling_part = magnitude * sign_flip
    root_scale = jnp.sqrt(diagonal_part)
    pair_index = ((0, 0, 1), (0, 0, 2), (1, 2, 0))
    rows_list = []
    for first in range(3):
        entries = []
        for second in range(3):
            if first == second:
                entries.append(diagonal_part[:, first, :])
            else:
                which = pair_index[min(first, second)][max(first, second)]
                entries.append(root_scale[:, first, :] * root_scale[:, second, :] * coupling_part[:, which, :])
        rows_list.append(jnp.stack(entries, axis=1))
    return jnp.stack(rows_list, axis=1).astype(jnp.float32)


def touch_ends(values, key, smallest, top_value):
    spot = [jax.random.randint(jax.random.fold_in(key, axis), (), 0, length) for axis, length in enumerate(values.shape)]
    longest = values.shape.index(max(values.shape))
    neighbour = spot[:longest] + [(spot[longest] + 1) % values.shape[longest]] + spot[longest + 1:]
    return values.at[tuple(spot)].set(smallest).at[tuple(neighbour)].set(top_value)


def block_levels(stream_key, extent, pieces, smallest, top_value):
    def one(dim, shards_of):
        heights = jax.random.uniform(jax.random.fold_in(jax.random.fold_in(stream_key, 6), dim), (shards_of,), jnp.float32, smallest / len(pieces), top_value / len(pieces))
        return jnp.repeat(jnp.exp(heights), extent[dim] // shards_of).reshape((-1,) + (1,) * (len(extent) - dim - 1))

    factor_of = one(*pieces[0])
    for cut in pieces[1:]:
        factor_of = factor_of * one(*cut)
    return factor_of


def noise(stream_key, dims, deviation, most, split=(), kind=jnp.bfloat16):
    values = deviation * jax.random.normal(stream_key, dims, jnp.float32)
    if split:
        values = values * block_levels(stream_key, dims, split, -0.22, 0.18)
    return jnp.clip(values, -most, most).astype(kind)


def setup_inputs(seed: int = 0) -> dict:
    key_list = jax.random.split(jax.random.key(seed), 6)
    return {
        "counts": draw_counts(jax.random.fold_in(key_list[5], 71), 0),
        "tiles": touch_ends(jax.random.randint(key_list[1], (CLUSTERS, CAM_DEVICES), 0, GT), jax.random.fold_in(key_list[1], 1), 0, GT - 1).astype(jnp.int32),
        "cam_jac": noise(key_list[2], (CLUSTERS, ROWS, CAMC), 0.1, 0.6, ((0, 8), (2, 4)), jnp.float32),
        "point_jac": noise(key_list[3], (CLUSTERS, ROWS, 3, PTS), (3 * PTS) ** -0.5, 0.15625, ((0, 8), (3, 4)), jnp.float32),
        "point_inv": draw_point_inv(jax.random.fold_in(key_list[5], 71), 0),
    }


HIGHEST_PRECISION = lax.Precision.HIGHEST


def contract_rows(left, right):
    return lax.dot_general(left, right, (((0,), (0,)), ((), ())), precision=HIGHEST_PRECISION, preferred_element_type=jnp.float32)


def reference(counts, tiles, cam_jac, point_jac, point_inv):
    tile_width = CAMC // CAM_DEVICES
    within = jnp.arange(tile_width, dtype=jnp.int32)
    groups = jnp.arange(CAM_DEVICES, dtype=jnp.int32)

    def add_cluster(accumulator, cluster):
        panel = cam_jac[cluster]
        points = point_jac[cluster]
        inverse = point_inv[cluster]
        live = ((cluster % SLOTS) < counts[cluster // SLOTS]).astype(jnp.float32)
        weighted = jnp.einsum('rjp,jkp->rkp', points, inverse, precision=HIGHEST_PRECISION)
        coupled = jnp.dot(weighted.reshape(ROWS, -1), points.reshape(ROWS, -1).T, precision=HIGHEST_PRECISION, preferred_element_type=jnp.float32)
        schur = contract_rows(panel, panel - jnp.dot(coupled, panel, precision=HIGHEST_PRECISION, preferred_element_type=jnp.float32)) * live
        global_tiles = (groups * GT + tiles[cluster]).astype(jnp.int32)
        position = (global_tiles[:, None] * tile_width + within[None, :]).reshape(-1).astype(jnp.int32)
        accumulator = accumulator.at[position[:, None], position[None, :]].add(schur)
        return accumulator, None

    start = jnp.zeros((CAMS, CAMS), jnp.float32)
    total, _ = lax.scan(add_cluster, start, jnp.arange(CLUSTERS, dtype=jnp.int32))
    return total.reshape(CAM_DEVICES, CAMS // CAM_DEVICES, CAMS)
```

```python
import functools
import itertools

import jax
import jax.numpy as jnp
from jax import lax
from jax.experimental import pallas as pl
from jax.experimental.pallas import tpu as pltpu
from jax.sharding import PartitionSpec as P

MESH = pl.DeviceIdType.MESH
ANY = pl.BlockSpec(memory_space=pl.ANY)
VMEM = pl.BlockSpec(memory_space=pltpu.VMEM)
SMEM = pl.BlockSpec(memory_space=pltpu.SMEM)
LANES = 128
GROUP_TILES = 4
VMEM_LIMIT = 56 * 1024 * 1024


def halves(x):
    high = x.astype(jnp.bfloat16)
    low = (x - high.astype(jnp.float32)).astype(jnp.bfloat16)
    return high, low


def dot3(left, right, dims):
    lh, ll = halves(left)
    rh, rl = halves(right)
    (ld,), (rd,) = dims
    return lax.dot_general(
        jnp.concatenate([lh, lh, ll], axis=ld),
        jnp.concatenate([rh, rl, rh], axis=rd),
        (dims, ((), ())),
        preferred_element_type=jnp.float32,
    )


def greet(peers):
    barrier = pltpu.get_barrier_semaphore()
    for peer in peers:
        pl.semaphore_signal(barrier, inc=1, device_id=peer, device_id_type=MESH)
    pl.semaphore_wait(barrier, len(peers))


def send(src, dst, send_sem, recv_sem, peer):
    return pltpu.make_async_remote_copy(
        src_ref=src, dst_ref=dst, send_sem=send_sem, recv_sem=recv_sem,
        device_id=peer, device_id_type=MESH,
    )


def exchange_kernel(
    jac, points, inv, others, coupled,
    points_here, outgoing, arrived, mine, across_in,
    send_sem, recv_sem, local_sem,
):
    camera = lax.axis_index("camera")
    core = lax.rem(camera, 2)
    sibling = {"camera": camera + 1 - 2 * core}
    across = {"camera": lax.rem(camera + 2, 4)}
    half = coupled.shape[0] // 2
    own, theirs = core * half, (1 - core) * half

    loads = [
        pltpu.make_async_copy(
            points.at[pl.ds(start, half)], points_here.at[which], local_sem.at[which]
        )
        for which, start in enumerate((theirs, own))
    ]
    for load in loads:
        load.start()
    greet([sibling, across])
    to_across = send(jac, others.at[1], send_sem.at[0], recv_sem.at[0], across)
    to_across.start()
    to_sibling = send(jac, others.at[0], send_sem.at[1], recv_sem.at[1], sibling)
    to_sibling.start()

    def couple(which, start, target):
        def body(i, carry):
            p = [points_here[which, i, :, j, :] for j in range(3)]
            w = [
                sum(p[j] * inv[start + i, j, k:k + 1, :] for j in range(3))
                for k in range(3)
            ]
            target[i] = dot3(
                jnp.concatenate(w, axis=1), jnp.concatenate(p, axis=1), (((1,), (1,)))
            )
            return carry

        loads[which].wait()
        lax.fori_loop(0, half, body, 0)

    couple(0, theirs, outgoing)
    part = send(outgoing, arrived, send_sem.at[2], recv_sem.at[2], sibling)
    part.start()
    couple(1, own, mine)
    part.wait_recv()
    mine[...] += arrived[...]
    cross = send(mine, across_in, send_sem.at[3], recv_sem.at[3], across)
    cross.start()
    to_across.wait_recv()
    forward = send(others.at[1], others.at[2], send_sem.at[4], recv_sem.at[4], sibling)
    forward.start()
    cross.wait_recv()
    block = coupled.at[pl.ds(own, half)]
    block[...] = mine[...] + across_in[...]
    back = send(block, block, send_sem.at[5], recv_sem.at[5], sibling)
    back.start()
    for copy in (to_across, to_sibling, part, cross):
        copy.wait_send()
    to_sibling.wait_recv()
    forward.wait()
    back.wait()


def exchange(jac, points, inv):
    slots, rows, width = jac.shape
    half = slots // 2
    block = pltpu.VMEM((half, rows, rows), jnp.float32)
    return pl.pallas_call(
        exchange_kernel,
        name="camera_exchange",
        out_shape=(
            jax.ShapeDtypeStruct((3, slots, rows, width), jnp.float32),
            jax.ShapeDtypeStruct((slots, rows, rows), jnp.float32),
        ),
        in_specs=[ANY, ANY, VMEM],
        out_specs=(ANY, VMEM),
        scratch_shapes=[
            pltpu.VMEM((2, half) + points.shape[1:], jnp.float32),
            block, block, block, block,
            pltpu.SemaphoreType.DMA((6,)),
            pltpu.SemaphoreType.DMA((6,)),
            pltpu.SemaphoreType.DMA((2,)),
        ],
        compiler_params=pltpu.CompilerParams(
            collective_id=0, has_side_effects=True, vmem_limit_bytes=VMEM_LIMIT
        ),
    )(jac, points, inv)


def schur_kernel(group_tiles, counts, tiles, jac, others, coupled, acc):
    camera = lax.axis_index("camera")
    device = lax.axis_index("cluster")
    slots, _, width = jac.shape
    wide = group_tiles * width
    live = counts[device]
    acc[...] = jnp.zeros_like(acc)

    def one(c):
        panel = jac[c]
        panels = [panel] + [others[r, c] for r in range(3)]
        left = panel - dot3(coupled[c], panel, (((1,), (0,))))
        left = left * jnp.where(c < live, 1.0, 0.0)
        return dot3(left, jnp.concatenate(panels, axis=1), (((0,), (0,))))

    def add(c, block):
        at = (device * slots + c) * 4
        row = pl.ds(pl.multiple_of(tiles[at + camera] * width, width), width)
        acc[row, 3 * wide:] += block[:, :width]
        for r in range(1, 4):
            tile = tiles[at + jnp.bitwise_xor(camera, r)]
            col = pl.multiple_of((r - 1) * wide + tile * width, width)
            acc[row, pl.ds(col, width)] += block[:, r * width:(r + 1) * width]

    def body(step, carry):
        blocks = [one(2 * step), one(2 * step + 1)]
        add(2 * step, blocks[0])
        add(2 * step + 1, blocks[1])
        return carry

    lax.fori_loop(0, (live + 1) // 2, body, 0)


def schur(counts, tiles, jac, others, coupled, group_tiles):
    width = jac.shape[2]
    wide = group_tiles * width
    return pl.pallas_call(
        functools.partial(schur_kernel, group_tiles),
        name="schur_sum",
        out_shape=jax.ShapeDtypeStruct((wide, 3 * wide + width), jnp.float32),
        in_specs=[SMEM, SMEM, VMEM, VMEM, VMEM],
        out_specs=VMEM,
        compiler_params=pltpu.CompilerParams(vmem_limit_bytes=VMEM_LIMIT),
    )(counts, tiles.reshape(-1), jac, others, coupled)


def parts_of(columns, bits):
    straight = tuple(range(bits))
    swapped = (1, 0) + straight[2:]
    tiles = columns // LANES
    cuts = [0, 3 * tiles // 8, 5 * tiles // 8 + 1, tiles]
    orders = [straight, swapped, straight]
    return [
        (cuts[i] * LANES, (cuts[i + 1] - cuts[i]) * LANES, orders[i]) for i in range(3)
    ]


def reduce_kernel(bits, parts, group_tiles, given, out, acc, *scratch):
    buffers, (send_sem, recv_sem, local_sem) = scratch[:-3], scratch[-3:]
    camera = lax.axis_index("camera")
    device = lax.axis_index("cluster")
    bit = [lax.rem(device // (1 << b), 2) for b in range(bits)]
    peer = [{"cluster": device + (1 - 2 * bit[b]) * (1 << b)} for b in range(bits)]
    loads = []
    for part, (first, width, _) in enumerate(parts):
        at = (slice(None),) * (bits + 1) + (pl.ds(first, width),)
        loads.append(pltpu.make_async_copy(given.at[at], acc.at[at], local_sem.at[part]))
        loads[-1].start()
    greet(peer)

    def region(part, step, flip):
        start, width, order = parts[part]
        index = [slice(None)] * bits
        for b in order[:step]:
            index[bits - 1 - b] = bit[b]
        b = order[step]
        index[bits - 1 - b] = 1 - bit[b] if flip else bit[b]
        return index, pl.ds(start, width)

    def start(part, step):
        index, columns = region(part, step, True)
        which = part * bits + step
        source = acc if step else given
        copy = send(
            source.at[tuple(index) + (slice(None), columns)], buffers[which],
            send_sem.at[which], recv_sem.at[which], peer[parts[part][2][step]],
        )
        copy.start()
        return copy

    copies = {(part, 0): start(part, 0) for part in range(len(parts))}
    for step in range(bits):
        for part in range(len(parts)):
            if step == 0:
                loads[part].wait()
            copies[part, step].wait_recv()
            index, columns = region(part, step, False)
            free = [i for i in range(bits) if isinstance(index[i], slice)]
            for place in itertools.product(range(2), repeat=len(free)):
                full = list(index)
                for i, value in zip(free, place):
                    full[i] = value
                at = tuple(full) + (slice(None), columns)
                acc[at] += buffers[part * bits + step][place]
            if step + 1 < bits:
                copies[part, step + 1] = start(part, step + 1)
    total = tuple(reversed(bit))
    rows, columns = out.shape
    wide = columns // 4
    mine = pl.multiple_of(camera * wide, wide)
    out[:, pl.ds(mine, wide)] = jnp.zeros((rows, wide), jnp.float32)
    tile = device * rows * group_tiles // wide
    width = wide // group_tiles
    out[:, pl.ds(pl.multiple_of(camera * wide + tile * width, width), width)] = acc[
        total + (slice(None), pl.ds(3 * wide, width))
    ]
    for r in range(1, 4):
        other = pl.multiple_of(jnp.bitwise_xor(camera, r) * wide, wide)
        out[:, pl.ds(other, wide)] = acc[total + (slice(None), pl.ds((r - 1) * wide, wide))]
    for copy in copies.values():
        copy.wait_send()


def reduce(acc, devices, group_tiles, cameras):
    wide, columns = acc.shape
    bits = devices.bit_length() - 1
    rows = wide // devices
    parts = parts_of(columns, bits)
    buffers = [
        pltpu.VMEM((2,) * (bits - 1 - step) + (rows, width), jnp.float32)
        for _, width, _ in parts
        for step in range(bits)
    ]
    count = len(buffers)
    return pl.pallas_call(
        functools.partial(reduce_kernel, bits, parts, group_tiles),
        name="cluster_reduce",
        out_shape=jax.ShapeDtypeStruct((rows, cameras * wide), jnp.float32),
        in_specs=[ANY],
        out_specs=VMEM,
        scratch_shapes=[pltpu.VMEM((2,) * bits + (rows, columns), jnp.float32)]
        + buffers
        + [pltpu.SemaphoreType.DMA((n,)) for n in (count, count, len(parts))],
        compiler_params=pltpu.CompilerParams(
            collective_id=1, has_side_effects=True, vmem_limit_bytes=VMEM_LIMIT
        ),
    )(acc.reshape((2,) * bits + (rows, columns)))


def on_device(counts, tiles, cam_jac, point_jac, point_inv):
    devices = lax.axis_size("cluster")
    cameras = lax.axis_size("camera")
    others, coupled = exchange(cam_jac, point_jac, point_inv)
    acc = schur(counts, tiles, cam_jac, others, coupled, GROUP_TILES)
    return reduce(acc, devices, GROUP_TILES, cameras)[None]


def solution(mesh):
    in_specs = (
        P(),
        P(),
        P("cluster", None, "camera"),
        P("cluster", None, None, "camera"),
        P("cluster", None, None, "camera"),
    )
    out_specs = P("camera", "cluster", None)
    return jax.shard_map(
        on_device,
        mesh=mesh, in_specs=in_specs, out_specs=out_specs, check_vma=False,
    )
```

```python
import functools
import itertools

import jax
import jax.numpy as jnp
from jax import lax
from jax.experimental import pallas as pl
from jax.experimental.pallas import tpu as pltpu
from jax.sharding import PartitionSpec as P

MESH = pl.DeviceIdType.MESH
ANY = pl.BlockSpec(memory_space=pl.ANY)
VMEM = pl.BlockSpec(memory_space=pltpu.VMEM)
SMEM = pl.BlockSpec(memory_space=pltpu.SMEM)
LANES = 128
GROUP_TILES = 4
VMEM_LIMIT = 56 * 1024 * 1024


def halves(x):
    high = x.astype(jnp.bfloat16)
    low = (x - high.astype(jnp.float32)).astype(jnp.bfloat16)
    return high, low


def dot3(left, right, dims):
    lh, ll = halves(left)
    rh, rl = halves(right)
    (ld,), (rd,) = dims
    return lax.dot_general(
        jnp.concatenate([lh, lh, ll], axis=ld),
        jnp.concatenate([rh, rl, rh], axis=rd),
        (dims, ((), ())),
        preferred_element_type=jnp.float32,
    )


def greet(peers):
    barrier = pltpu.get_barrier_semaphore()
    for peer in peers:
        pl.semaphore_signal(barrier, inc=1, device_id=peer, device_id_type=MESH)
    pl.semaphore_wait(barrier, len(peers))


def send(src, dst, send_sem, recv_sem, peer):
    return pltpu.make_async_remote_copy(
        src_ref=src, dst_ref=dst, send_sem=send_sem, recv_sem=recv_sem,
        device_id=peer, device_id_type=MESH,
    )


def exchange_kernel(
    jac, points, inv, near, far, coupled,
    points_here, outgoing, arrived, mine, across_in,
    send_sem, recv_sem, local_sem,
):
    camera = lax.axis_index("camera")
    core = lax.rem(camera, 2)
    sibling = {"camera": camera + 1 - 2 * core}
    across = {"camera": lax.rem(camera + 2, 4)}
    half = coupled.shape[0] // 2
    own, theirs = core * half, (1 - core) * half

    loads = [
        pltpu.make_async_copy(
            points.at[pl.ds(start, half)], points_here.at[which], local_sem.at[which]
        )
        for which, start in enumerate((theirs, own))
    ]
    for load in loads:
        load.start()
    greet([sibling, across])
    early = jac.at[pl.ds(0, far.shape[1])]
    to_across = send(early, far.at[0], send_sem.at[0], recv_sem.at[0], across)
    to_across.start()
    to_sibling = send(jac, near, send_sem.at[1], recv_sem.at[1], sibling)
    to_sibling.start()

    def couple(which, start, target):
        def body(i, carry):
            p = [points_here[which, i, j] for j in range(3)]
            w = [
                sum(p[j] * inv[j, k, pl.ds(start + i, 1), :] for j in range(3))
                for k in range(3)
            ]
            target[i] = dot3(
                jnp.concatenate(w, axis=1), jnp.concatenate(p, axis=1), (((1,), (1,)))
            )
            return carry

        loads[which].wait()
        lax.fori_loop(0, half, body, 0)

    couple(0, theirs, outgoing)
    part = send(outgoing, arrived, send_sem.at[2], recv_sem.at[2], sibling)
    part.start()
    couple(1, own, mine)
    part.wait_recv()
    mine[...] += arrived[...]
    cross = send(mine, across_in, send_sem.at[3], recv_sem.at[3], across)
    cross.start()
    to_across.wait_recv()
    forward = send(far.at[0], far.at[1], send_sem.at[4], recv_sem.at[4], sibling)
    forward.start()
    cross.wait_recv()
    block = coupled.at[pl.ds(own, half)]
    block[...] = mine[...] + across_in[...]
    back = send(block, block, send_sem.at[5], recv_sem.at[5], sibling)
    back.start()
    for copy in (to_across, to_sibling, part, cross):
        copy.wait_send()
    to_sibling.wait_recv()
    forward.wait()
    back.wait()


def exchange(jac, points, inv):
    slots, rows, width = jac.shape
    half = slots // 2
    block = pltpu.VMEM((half, rows, rows), jnp.float32)
    return pl.pallas_call(
        exchange_kernel,
        name="camera_exchange",
        out_shape=(
            jax.ShapeDtypeStruct((slots, rows, width), jnp.float32),
            jax.ShapeDtypeStruct((2, half, rows, width), jnp.float32),
            jax.ShapeDtypeStruct((slots, rows, rows), jnp.float32),
        ),
        in_specs=[ANY, ANY, VMEM],
        out_specs=(ANY, ANY, VMEM),
        scratch_shapes=[
            pltpu.VMEM((2, half) + points.shape[1:], jnp.float32),
            block, block, block, block,
            pltpu.SemaphoreType.DMA((6,)),
            pltpu.SemaphoreType.DMA((6,)),
            pltpu.SemaphoreType.DMA((2,)),
        ],
        compiler_params=pltpu.CompilerParams(
            collective_id=0, has_side_effects=True, vmem_limit_bytes=VMEM_LIMIT
        ),
    )(jac, points, inv)


def add_pair(tiles, acc, slot, camera, r, first, width, block):
    other = jnp.bitwise_xor(camera, r)
    row_tile, col_tile = tiles[camera, slot], tiles[other, slot]
    upper = (camera > other).astype(jnp.int32)

    @pl.when(lax.rem(row_tile + col_tile + upper, 2) == 0)
    def _():
        row = pl.ds(pl.multiple_of(row_tile * width, width), width)
        col = pl.multiple_of(first + (col_tile // 2) * width, width)
        acc[row, pl.ds(col, width)] += block


def near_kernel(counts, tiles, jac, near, coupled, acc, left):
    camera = lax.axis_index("camera")
    device = lax.axis_index("cluster")
    slots, _, width = jac.shape
    live = counts[device]
    acc[...] = jnp.zeros_like(acc)

    def one(c):
        panel = jac[c]
        schur = panel - dot3(coupled[c], panel, (((1,), (0,))))
        schur = schur * jnp.where(c < live, 1.0, 0.0)
        left[c] = schur
        return dot3(schur, jnp.concatenate([panel, near[c]], axis=1), (((0,), (0,))))

    def add(c, block):
        slot = device * slots + c
        row = pl.ds(pl.multiple_of(tiles[camera, slot] * width, width), width)
        acc[row, :width] += block[:, :width]
        add_pair(tiles, acc, slot, camera, 1, width, width, block[:, width:])

    def body(step, carry):
        blocks = [one(2 * step), one(2 * step + 1)]
        add(2 * step, blocks[0])
        add(2 * step + 1, blocks[1])
        return carry

    lax.fori_loop(0, (live + 1) // 2, body, 0)


def near_sum(counts, tiles, jac, near, coupled):
    slots, rows, width = jac.shape
    return pl.pallas_call(
        near_kernel,
        name="near_sum",
        out_shape=(
            jax.ShapeDtypeStruct(
                (GROUP_TILES * width, (1 + GROUP_TILES // 2) * width), jnp.float32
            ),
            jax.ShapeDtypeStruct((slots, rows, width), jnp.float32),
        ),
        in_specs=[SMEM, SMEM, VMEM, VMEM, VMEM],
        out_specs=(VMEM, VMEM),
        compiler_params=pltpu.CompilerParams(vmem_limit_bytes=VMEM_LIMIT),
    )(counts, tiles, jac, near, coupled)


def far_kernel(counts, tiles, left, early, late, acc):
    camera = lax.axis_index("camera")
    device = lax.axis_index("cluster")
    slots, _, width = left.shape
    half = early.shape[1]
    live = counts[device]
    acc[...] = jnp.zeros_like(acc)

    def part(far, base, steps):
        def one(i):
            right = jnp.concatenate([far[0, i], far[1, i]], axis=1)
            return dot3(left[base + i], right, (((0,), (0,))))

        def add(i, block):
            slot = device * slots + base + i
            for r in (2, 3):
                cut = block[:, (r - 2) * width:(r - 1) * width]
                first = (r - 2) * (GROUP_TILES // 2) * width
                add_pair(tiles, acc, slot, camera, r, first, width, cut)

        def body(step, carry):
            blocks = [one(2 * step), one(2 * step + 1)]
            add(2 * step, blocks[0])
            add(2 * step + 1, blocks[1])
            return carry

        lax.fori_loop(0, steps, body, 0)

    steps = (live + 1) // 2
    part(early, 0, jnp.minimum(steps, half // 2))
    part(late, half, jnp.maximum(steps - half // 2, 0))


def far_sum(counts, tiles, left, early, late):
    width = left.shape[2]
    return pl.pallas_call(
        far_kernel,
        name="far_sum",
        out_shape=jax.ShapeDtypeStruct(
            (GROUP_TILES * width, GROUP_TILES * width), jnp.float32
        ),
        in_specs=[SMEM, SMEM, VMEM, VMEM, VMEM],
        out_specs=VMEM,
        compiler_params=pltpu.CompilerParams(vmem_limit_bytes=VMEM_LIMIT),
    )(counts, tiles, left, early, late)


class Reduction:
    def __init__(self, bits, width, orders, given, acc, buffers, sems):
        self.bits, self.width, self.orders = bits, width, orders
        self.given, self.acc, self.buffers = given, acc, buffers
        self.send_sem, self.recv_sem, self.local_sem = sems
        device = lax.axis_index("cluster")
        self.bit = [lax.rem(device // (1 << b), 2) for b in range(bits)]
        self.peers = [
            {"cluster": device + (1 - 2 * self.bit[b]) * (1 << b)} for b in range(bits)
        ]
        self.copies = {}

    def load(self):
        self.loads = []
        for part in range(len(self.orders)):
            at = (slice(None),) * (self.bits + 1) + (self.columns(part),)
            copy = pltpu.make_async_copy(
                self.given.at[at], self.acc.at[at], self.local_sem.at[part]
            )
            copy.start()
            self.loads.append(copy)

    def columns(self, part):
        return pl.ds(part * self.width, self.width)

    def region(self, part, step, flip):
        index = [slice(None)] * self.bits
        order = self.orders[part]
        for b in order[:step]:
            index[self.bits - 1 - b] = self.bit[b]
        b = order[step]
        index[self.bits - 1 - b] = 1 - self.bit[b] if flip else self.bit[b]
        return index

    def start(self, part, step):
        which = part * self.bits + step
        source = self.acc if step else self.given
        index = tuple(self.region(part, step, True))
        copy = send(
            source.at[index + (slice(None), self.columns(part))], self.buffers[which],
            self.send_sem.at[which], self.recv_sem.at[which],
            self.peers[self.orders[part][step]],
        )
        copy.start()
        self.copies[part, step] = copy

    def begin(self):
        for part in range(len(self.orders)):
            self.start(part, 0)

    def run(self, finished):
        for step in range(self.bits):
            for part in range(len(self.orders)):
                if step == 0:
                    self.loads[part].wait()
                self.copies[part, step].wait_recv()
                index = self.region(part, step, False)
                free = [i for i in range(self.bits) if isinstance(index[i], slice)]
                for place in itertools.product(range(2), repeat=len(free)):
                    full = list(index)
                    for i, value in zip(free, place):
                        full[i] = value
                    at = tuple(full) + (slice(None), self.columns(part))
                    self.acc[at] += self.buffers[part * self.bits + step][place]
                if step + 1 < self.bits:
                    self.start(part, step + 1)
                else:
                    finished(part, tuple(reversed(self.bit)) + (slice(None), self.columns(part)))

    def end(self):
        for copy in self.copies.values():
            copy.wait_send()


def reduction_scratch(bits, rows, width, parts):
    count = parts * bits
    return (
        [pltpu.VMEM((2,) * bits + (rows, parts * width), jnp.float32)]
        + [
            pltpu.VMEM((2,) * (bits - 1 - step) + (rows, width), jnp.float32)
            for _ in range(parts)
            for step in range(bits)
        ]
        + [pltpu.SemaphoreType.DMA((n,)) for n in (count, count, parts)]
    )


def orders_of(bits, parts):
    straight = tuple(range(bits))
    swapped = (1, 0) + straight[2:]
    return [swapped if part == 1 else straight for part in range(parts)]


def near_reduce_kernel(bits, width, given, jac, out, far, acc, *scratch):
    parts = out.shape[1] // width
    buffers, sems = scratch[:parts * bits], scratch[parts * bits:-2]
    send_sem, recv_sem = scratch[-2:]
    camera = lax.axis_index("camera")
    sibling = {"camera": camera + 1 - 2 * lax.rem(camera, 2)}
    across = {"camera": lax.rem(camera + 2, 4)}
    work = Reduction(bits, width, orders_of(bits, parts), given, acc, buffers, sems)
    work.load()
    greet(work.peers + [sibling, across])
    work.begin()
    late = far.shape[1]
    to_across = send(
        jac.at[pl.ds(jac.shape[0] - late, late)], far.at[0],
        send_sem.at[0], recv_sem.at[0], across,
    )
    to_across.start()

    def finished(part, at):
        out[:, part * width:(part + 1) * width] = acc[at]

    work.run(finished)
    to_across.wait_recv()
    forward = send(far.at[0], far.at[1], send_sem.at[1], recv_sem.at[1], sibling)
    forward.start()
    work.end()
    to_across.wait_send()
    forward.wait()


def near_reduce(acc, jac, devices):
    wide, columns = acc.shape
    slots, depth, width = jac.shape
    bits = devices.bit_length() - 1
    rows = wide // devices
    return pl.pallas_call(
        functools.partial(near_reduce_kernel, bits, width),
        name="near_reduce",
        out_shape=(
            jax.ShapeDtypeStruct((rows, columns), jnp.float32),
            jax.ShapeDtypeStruct((2, slots - slots // 2, depth, width), jnp.float32),
        ),
        in_specs=[ANY, ANY],
        out_specs=(VMEM, ANY),
        scratch_shapes=reduction_scratch(bits, rows, width, columns // width)
        + [pltpu.SemaphoreType.DMA((2,)), pltpu.SemaphoreType.DMA((2,))],
        compiler_params=pltpu.CompilerParams(
            collective_id=1, has_side_effects=True, vmem_limit_bytes=VMEM_LIMIT
        ),
    )(acc.reshape((2,) * bits + (rows, columns)), jac)


def far_reduce_kernel(bits, width, given, near, out, acc, *scratch):
    parts = GROUP_TILES
    pairs = GROUP_TILES // 2
    buffers, sems = scratch[:parts * bits], scratch[parts * bits:-4]
    strips, traded, send_sem, recv_sem = scratch[-4:]
    camera = lax.axis_index("camera")
    device = lax.axis_index("cluster")
    rows = out.shape[0]
    shares = width // rows
    tile, place = device // shares, lax.rem(device, shares)
    work = Reduction(bits, width, orders_of(bits, parts), given, acc, buffers, sems)
    work.load()

    other = [jnp.bitwise_xor(camera, r) for r in range(4)]
    parity = [lax.rem(tile + (camera > other[r]).astype(jnp.int32), 2) for r in range(4)]
    barrier = pltpu.get_barrier_semaphore()
    for peer in work.peers:
        pl.semaphore_signal(barrier, inc=1, device_id=peer, device_id_type=MESH)
    for r in range(1, 4):
        for k in range(pairs):
            for d in range(shares):
                peer = {
                    "camera": other[r], "cluster": (2 * k + 1 - parity[r]) * shares + d
                }
                pl.semaphore_signal(barrier, inc=1, device_id=peer, device_id_type=MESH)
    pl.semaphore_wait(barrier, bits + 3 * pairs * shares)

    trades = []

    def trade(r, k):
        for d in range(shares):
            copy = send(
                strips.at[r - 1, k],
                traded.at[r - 1, tile // 2, pl.ds(place * rows, rows)],
                send_sem.at[((r - 1) * pairs + k) * shares + d], recv_sem.at[r - 1],
                {"camera": other[r], "cluster": (2 * k + parity[r]) * shares + d},
            )
            copy.start()
            trades.append(copy)

    def column(r, t):
        return pl.ds(pl.multiple_of((other[r] * GROUP_TILES + t) * width, width), width)

    work.begin()
    for k in range(pairs):
        strips[0, k] = near[:, (1 + k) * width:(2 + k) * width]
        trade(1, k)
    for t in range(GROUP_TILES):
        out[:, column(0, t)] = jnp.where(t == tile, near[:, :width], 0.0)

    def finished(part, at):
        r, k = 2 + part // pairs, part % pairs
        strips[r - 1, k] = acc[at]
        trade(r, k)

    work.run(finished)
    for r in range(1, 4):
        pltpu.make_async_copy(traded.at[r - 1], traded.at[r - 1], recv_sem.at[r - 1]).wait()
        for k in range(pairs):
            out[:, column(r, 2 * k + parity[r])] = strips[r - 1, k]
            turned = traded[r - 1, k].T
            kept = turned[:rows]
            for d in range(1, shares):
                kept = jnp.where(place == d, turned[d * rows:(d + 1) * rows], kept)
            out[:, column(r, 2 * k + 1 - parity[r])] = kept
    work.end()
    for copy in trades:
        copy.wait_send()


def far_reduce(acc, near, devices, cameras, width):
    wide, columns = acc.shape
    bits = devices.bit_length() - 1
    rows = wide // devices
    pairs = GROUP_TILES // 2
    return pl.pallas_call(
        functools.partial(far_reduce_kernel, bits, width),
        name="far_reduce",
        out_shape=jax.ShapeDtypeStruct((rows, cameras * wide), jnp.float32),
        in_specs=[ANY, VMEM],
        out_specs=VMEM,
        scratch_shapes=reduction_scratch(bits, rows, width, columns // width)
        + [
            pltpu.VMEM((3, pairs, rows, width), jnp.float32),
            pltpu.VMEM((3, pairs, width, width), jnp.float32),
            pltpu.SemaphoreType.DMA((3 * pairs * width // rows,)),
            pltpu.SemaphoreType.DMA((3,)),
        ],
        compiler_params=pltpu.CompilerParams(
            collective_id=2, has_side_effects=True, vmem_limit_bytes=VMEM_LIMIT
        ),
    )(acc.reshape((2,) * bits + (rows, columns)), near)


def on_device(counts, tiles, cam_jac, point_jac, point_inv):
    devices = lax.axis_size("cluster")
    cameras = lax.axis_size("camera")
    width = cam_jac.shape[2]
    tiles = tiles.T
    near, early, coupled = exchange(
        cam_jac, point_jac.transpose(0, 2, 1, 3), point_inv.transpose(1, 2, 0, 3)
    )
    near_acc, left = near_sum(counts, tiles, cam_jac, near, coupled)
    near_strip, late = near_reduce(near_acc, cam_jac, devices)
    far_acc = far_sum(counts, tiles, left, early, late)
    return far_reduce(far_acc, near_strip, devices, cameras, width)[None]


def solution(mesh):
    in_specs = (
        P(),
        P(),
        P("cluster", None, "camera"),
        P("cluster", None, None, "camera"),
        P("cluster", None, None, "camera"),
    )
    out_specs = P("camera", "cluster", None)
    return jax.shard_map(
        on_device,
        mesh=mesh, in_specs=in_specs, out_specs=out_specs, check_vma=False,
    )
```

```python
import functools
import itertools

import jax
import jax.numpy as jnp
from jax import lax
from jax.experimental import pallas as pl
from jax.experimental.pallas import tpu as pltpu
from jax.sharding import PartitionSpec as P

MESH = pl.DeviceIdType.MESH
ANY = pl.BlockSpec(memory_space=pl.ANY)
VMEM = pl.BlockSpec(memory_space=pltpu.VMEM)
SMEM = pl.BlockSpec(memory_space=pltpu.SMEM)
LANES = 128
GROUP_TILES = 4
STRIDE = 4
CHUNKS = 3
VMEM_LIMIT = 56 * 1024 * 1024


def halves(x):
    high = x.astype(jnp.bfloat16)
    low = (x - high.astype(jnp.float32)).astype(jnp.bfloat16)
    return high, low


def dot3(left, right, dims):
    lh, ll = halves(left)
    rh, rl = halves(right)
    (ld,), (rd,) = dims
    return lax.dot_general(
        jnp.concatenate([lh, lh, ll], axis=ld),
        jnp.concatenate([rh, rl, rh], axis=rd),
        (dims, ((), ())),
        preferred_element_type=jnp.float32,
    )


def greet(peers):
    barrier = pltpu.get_barrier_semaphore()
    for peer in peers:
        pl.semaphore_signal(barrier, inc=1, device_id=peer, device_id_type=MESH)
    pl.semaphore_wait(barrier, len(peers))


def send(src, dst, send_sem, recv_sem, peer):
    return pltpu.make_async_remote_copy(
        src_ref=src, dst_ref=dst, send_sem=send_sem, recv_sem=recv_sem,
        device_id=peer, device_id_type=MESH,
    )


def exchange_kernel(
    jac, points, inv, near, far, coupled,
    points_here, outgoing, arrived, mine, across_in,
    send_sem, recv_sem, local_sem,
):
    camera = lax.axis_index("camera")
    core = lax.rem(camera, 2)
    sibling = {"camera": camera + 1 - 2 * core}
    across = {"camera": lax.rem(camera + 2, 4)}
    half = coupled.shape[0] // 2
    quarter = half // 2
    own, theirs = core * half, (1 - core) * half
    starts = [theirs, own, theirs + quarter, own + quarter]

    loads = [
        pltpu.make_async_copy(
            points.at[pl.ds(start, quarter)], points_here.at[which], local_sem.at[which]
        )
        for which, start in enumerate(starts)
    ]
    for load in loads:
        load.start()
    greet([sibling, across])

    def copy_to(which, src, dst, peer):
        copy = send(src, dst, send_sem.at[which], recv_sem.at[which], peer)
        copy.start()
        return copy

    to_across = copy_to(0, jac.at[pl.ds(0, far.shape[1])], far.at[0], across)
    to_sibling = copy_to(1, jac, near, sibling)

    def couple(which, target):
        def body(i, carry):
            p = [points_here[which, i, j] for j in range(3)]
            w = [
                sum(p[j] * inv[j, k, pl.ds(starts[which] + i, 1), :] for j in range(3))
                for k in range(3)
            ]
            target[which // 2, i] = dot3(
                jnp.concatenate(w, axis=1), jnp.concatenate(p, axis=1), (((1,), (1,)))
            )
            return carry

        loads[which].wait()
        lax.fori_loop(0, quarter, body, 0, unroll=2)

    sent, crossed, returned = [], [], []
    for q in range(2):
        couple(2 * q, outgoing)
        sent.append(copy_to(2 + q, outgoing.at[q], arrived.at[q], sibling))
        couple(2 * q + 1, mine)
        sent[q].wait_recv()
        mine[q] += arrived[q]
        crossed.append(copy_to(4 + q, mine.at[q], across_in.at[q], across))
    to_across.wait_recv()
    forward = copy_to(6, far.at[0], far.at[1], sibling)
    for q in range(2):
        crossed[q].wait_recv()
        block = coupled.at[pl.ds(own + q * quarter, quarter)]
        block[...] = mine[q] + across_in[q]
        returned.append(copy_to(7 + q, block, block, sibling))
    for copy in [to_across, to_sibling] + sent + crossed:
        copy.wait_send()
    to_sibling.wait_recv()
    forward.wait()
    for copy in returned:
        copy.wait()


def exchange(jac, points, inv):
    slots, rows, width = jac.shape
    quarter = slots // 4
    block = pltpu.VMEM((2, quarter, rows, rows), jnp.float32)
    return pl.pallas_call(
        exchange_kernel,
        name="camera_exchange",
        out_shape=(
            jax.ShapeDtypeStruct((slots, rows, width), jnp.float32),
            jax.ShapeDtypeStruct((2, quarter, rows, width), jnp.float32),
            jax.ShapeDtypeStruct((slots, rows, rows), jnp.float32),
        ),
        in_specs=[ANY, ANY, VMEM],
        out_specs=(ANY, ANY, VMEM),
        scratch_shapes=[
            pltpu.VMEM((4, quarter) + points.shape[1:], jnp.float32),
            block, block, block, block,
            pltpu.SemaphoreType.DMA((9,)),
            pltpu.SemaphoreType.DMA((9,)),
            pltpu.SemaphoreType.DMA((4,)),
        ],
        compiler_params=pltpu.CompilerParams(
            collective_id=0, has_side_effects=True, vmem_limit_bytes=VMEM_LIMIT
        ),
    )(jac, points, inv)


def add_pair(tiles, acc, slot, camera, r, first, width, block):
    other = jnp.bitwise_xor(camera, r)
    row_tile, col_tile = tiles[camera, slot], tiles[other, slot]
    upper = (camera > other).astype(jnp.int32)

    @pl.when(lax.rem(row_tile + col_tile + upper, 2) == 0)
    def _():
        row = pl.ds(pl.multiple_of(row_tile * width, width), width)
        col = pl.multiple_of(first + (col_tile // 2) * width, width)
        acc[row, pl.ds(col, width)] += block


def near_kernel(counts, tiles, jac, near, coupled, acc, left):
    camera = lax.axis_index("camera")
    device = lax.axis_index("cluster")
    slots, _, width = jac.shape
    live = counts[device]
    acc[...] = jnp.zeros_like(acc)

    def one(c):
        panel = jac[c]
        schur = panel - dot3(coupled[c], panel, (((1,), (0,))))
        schur = schur * jnp.where(c < live, 1.0, 0.0)
        left[c] = schur
        return dot3(schur, jnp.concatenate([panel, near[c]], axis=1), (((0,), (0,))))

    def add(c, block):
        slot = device * slots + c
        row = pl.ds(pl.multiple_of(tiles[camera, slot] * width, width), width)
        acc[row, :width] += block[:, :width]
        add_pair(tiles, acc, slot, camera, 1, width, width, block[:, width:])

    def body(step, carry):
        blocks = [one(STRIDE * step + i) for i in range(STRIDE)]
        for i in range(STRIDE):
            add(STRIDE * step + i, blocks[i])
        return carry

    lax.fori_loop(0, (live + STRIDE - 1) // STRIDE, body, 0)


def near_sum(counts, tiles, jac, near, coupled):
    slots, rows, width = jac.shape
    return pl.pallas_call(
        near_kernel,
        name="near_sum",
        out_shape=(
            jax.ShapeDtypeStruct(
                (GROUP_TILES * width, (1 + GROUP_TILES // 2) * width), jnp.float32
            ),
            jax.ShapeDtypeStruct((slots, rows, width), jnp.float32),
        ),
        in_specs=[SMEM, SMEM, VMEM, VMEM, VMEM],
        out_specs=(VMEM, VMEM),
        compiler_params=pltpu.CompilerParams(vmem_limit_bytes=VMEM_LIMIT),
    )(counts, tiles, jac, near, coupled)


def far_kernel(counts, tiles, left, early, late, acc):
    camera = lax.axis_index("camera")
    device = lax.axis_index("cluster")
    slots, _, width = left.shape
    first = early.shape[1]
    live = counts[device]
    acc[...] = jnp.zeros_like(acc)

    def part(far, base, steps):
        def one(i):
            right = jnp.concatenate([far[0, i], far[1, i]], axis=1)
            return dot3(left[base + i], right, (((0,), (0,))))

        def add(i, block):
            slot = device * slots + base + i
            for r in (2, 3):
                cut = block[:, (r - 2) * width:(r - 1) * width]
                column = (r - 2) * (GROUP_TILES // 2) * width
                add_pair(tiles, acc, slot, camera, r, column, width, cut)

        def body(step, carry):
            blocks = [one(STRIDE * step + i) for i in range(STRIDE)]
            for i in range(STRIDE):
                add(STRIDE * step + i, blocks[i])
            return carry

        lax.fori_loop(0, steps, body, 0)

    steps = (live + STRIDE - 1) // STRIDE
    part(early, 0, jnp.minimum(steps, first // STRIDE))
    part(late, first, jnp.maximum(steps - first // STRIDE, 0))


def far_sum(counts, tiles, left, early, late):
    width = left.shape[2]
    return pl.pallas_call(
        far_kernel,
        name="far_sum",
        out_shape=jax.ShapeDtypeStruct(
            (GROUP_TILES * width, GROUP_TILES * width), jnp.float32
        ),
        in_specs=[SMEM, SMEM, VMEM, VMEM, VMEM],
        out_specs=VMEM,
        compiler_params=pltpu.CompilerParams(vmem_limit_bytes=VMEM_LIMIT),
    )(counts, tiles, left, early, late)


class Reduction:
    def __init__(self, bits, width, orders, given, acc, buffers, sems):
        self.bits, self.width, self.orders = bits, width, orders
        self.given, self.acc, self.buffers = given, acc, buffers
        self.send_sem, self.recv_sem, self.local_sem = sems
        device = lax.axis_index("cluster")
        self.bit = [lax.rem(device // (1 << b), 2) for b in range(bits)]
        self.peers = [
            {"cluster": device + (1 - 2 * self.bit[b]) * (1 << b)} for b in range(bits)
        ]
        self.copies = {}

    def load(self):
        self.loads = []
        for part in range(len(self.orders)):
            at = (slice(None),) * (self.bits + 1) + (self.columns(part),)
            copy = pltpu.make_async_copy(
                self.given.at[at], self.acc.at[at], self.local_sem.at[part]
            )
            copy.start()
            self.loads.append(copy)

    def columns(self, part):
        return pl.ds(part * self.width, self.width)

    def region(self, part, step, flip):
        index = [slice(None)] * self.bits
        order = self.orders[part]
        for b in order[:step]:
            index[self.bits - 1 - b] = self.bit[b]
        b = order[step]
        index[self.bits - 1 - b] = 1 - self.bit[b] if flip else self.bit[b]
        return index

    def start(self, part, step):
        which = part * self.bits + step
        source = self.acc if step else self.given
        index = tuple(self.region(part, step, True))
        copy = send(
            source.at[index + (slice(None), self.columns(part))], self.buffers[which],
            self.send_sem.at[which], self.recv_sem.at[which],
            self.peers[self.orders[part][step]],
        )
        copy.start()
        self.copies[part, step] = copy

    def begin(self):
        for part in range(len(self.orders)):
            self.start(part, 0)

    def run(self, finished, between=lambda step: None):
        for step in range(self.bits):
            for part in range(len(self.orders)):
                if step == 0:
                    self.loads[part].wait()
                self.copies[part, step].wait_recv()
                index = self.region(part, step, False)
                free = [i for i in range(self.bits) if isinstance(index[i], slice)]
                for place in itertools.product(range(2), repeat=len(free)):
                    full = list(index)
                    for i, value in zip(free, place):
                        full[i] = value
                    at = tuple(full) + (slice(None), self.columns(part))
                    self.acc[at] += self.buffers[part * self.bits + step][place]
                if step + 1 < self.bits:
                    self.start(part, step + 1)
                else:
                    finished(part, tuple(reversed(self.bit)) + (slice(None), self.columns(part)))
            between(step)

    def end(self):
        for copy in self.copies.values():
            copy.wait_send()


def reduction_scratch(bits, rows, width, parts):
    count = parts * bits
    return (
        [pltpu.VMEM((2,) * bits + (rows, parts * width), jnp.float32)]
        + [
            pltpu.VMEM((2,) * (bits - 1 - step) + (rows, width), jnp.float32)
            for _ in range(parts)
            for step in range(bits)
        ]
        + [pltpu.SemaphoreType.DMA((n,)) for n in (count, count, parts)]
    )


def orders_of(bits, parts):
    straight = tuple(range(bits))
    swapped = (1, 0) + straight[2:]
    far_first = (bits - 1,) + straight[:-1]
    if parts % 2:
        return [(straight, swapped, far_first)[part % 3] for part in range(parts)]
    return [(straight, swapped)[part % 2] for part in range(parts)]


def near_reduce_kernel(bits, width, given, jac, out, far, acc, *scratch):
    parts = out.shape[1] // width
    buffers, sems = scratch[:parts * bits], scratch[parts * bits:-2]
    send_sem, recv_sem = scratch[-2:]
    camera = lax.axis_index("camera")
    sibling = {"camera": camera + 1 - 2 * lax.rem(camera, 2)}
    across = {"camera": lax.rem(camera + 2, 4)}
    work = Reduction(bits, width, orders_of(bits, parts), given, acc, buffers, sems)
    work.load()
    greet(work.peers + [sibling, across])
    work.begin()
    late = far.shape[1]
    chunk = late // CHUNKS
    to_across, forwards = [], []
    for i in range(CHUNKS):
        to_across.append(send(
            jac.at[pl.ds(jac.shape[0] - late + i * chunk, chunk)],
            far.at[0, pl.ds(i * chunk, chunk)],
            send_sem.at[i], recv_sem.at[i], across,
        ))
        to_across[i].start()

    def forward(i):
        to_across[i].wait_recv()
        part = pl.ds(i * chunk, chunk)
        forwards.append(send(
            far.at[0, part], far.at[1, part],
            send_sem.at[CHUNKS + i], recv_sem.at[CHUNKS + i], sibling,
        ))
        forwards[i].start()

    def finished(part, at):
        out[:, part * width:(part + 1) * width] = acc[at]

    def between(step):
        if 1 <= step <= CHUNKS:
            forward(step - 1)

    work.run(finished, between)
    for i in range(len(forwards), CHUNKS):
        forward(i)
    work.end()
    for copy in to_across:
        copy.wait_send()
    for copy in forwards:
        copy.wait()


def near_reduce(acc, jac, devices):
    wide, columns = acc.shape
    slots, depth, width = jac.shape
    bits = devices.bit_length() - 1
    rows = wide // devices
    return pl.pallas_call(
        functools.partial(near_reduce_kernel, bits, width),
        name="near_reduce",
        out_shape=(
            jax.ShapeDtypeStruct((rows, columns), jnp.float32),
            jax.ShapeDtypeStruct((2, slots - slots // 4, depth, width), jnp.float32),
        ),
        in_specs=[ANY, ANY],
        out_specs=(VMEM, ANY),
        scratch_shapes=reduction_scratch(bits, rows, width, columns // width)
        + [pltpu.SemaphoreType.DMA((2 * CHUNKS,))] * 2,
        compiler_params=pltpu.CompilerParams(
            collective_id=1, has_side_effects=True, vmem_limit_bytes=VMEM_LIMIT
        ),
    )(acc.reshape((2,) * bits + (rows, columns)), jac)


def far_reduce_kernel(bits, width, given, near, out, acc, *scratch):
    parts = GROUP_TILES
    pairs = GROUP_TILES // 2
    buffers, sems = scratch[:parts * bits], scratch[parts * bits:-4]
    strips, traded, send_sem, recv_sem = scratch[-4:]
    camera = lax.axis_index("camera")
    device = lax.axis_index("cluster")
    rows = out.shape[0]
    shares = width // rows
    tile, place = device // shares, lax.rem(device, shares)
    work = Reduction(bits, width, orders_of(bits, parts), given, acc, buffers, sems)
    work.load()

    other = [jnp.bitwise_xor(camera, r) for r in range(4)]
    parity = [lax.rem(tile + (camera > other[r]).astype(jnp.int32), 2) for r in range(4)]
    barrier = pltpu.get_barrier_semaphore()
    for peer in work.peers:
        pl.semaphore_signal(barrier, inc=1, device_id=peer, device_id_type=MESH)
    for r in range(1, 4):
        for k in range(pairs):
            for d in range(shares):
                peer = {
                    "camera": other[r], "cluster": (2 * k + 1 - parity[r]) * shares + d
                }
                pl.semaphore_signal(barrier, inc=1, device_id=peer, device_id_type=MESH)
    pl.semaphore_wait(barrier, bits + 3 * pairs * shares)

    trades = []

    def trade(r, k):
        for d in range(shares):
            copy = send(
                strips.at[r - 1, k],
                traded.at[r - 1, tile // 2, pl.ds(place * rows, rows)],
                send_sem.at[((r - 1) * pairs + k) * shares + d], recv_sem.at[r - 1],
                {"camera": other[r], "cluster": (2 * k + parity[r]) * shares + d},
            )
            copy.start()
            trades.append(copy)

    def column(r, t):
        return pl.ds(pl.multiple_of((other[r] * GROUP_TILES + t) * width, width), width)

    work.begin()
    for k in range(pairs):
        strips[0, k] = near[:, (1 + k) * width:(2 + k) * width]
        trade(1, k)
    for t in range(GROUP_TILES):
        out[:, column(0, t)] = jnp.where(t == tile, near[:, :width], 0.0)

    def finished(part, at):
        r, k = 2 + part // pairs, part % pairs
        strips[r - 1, k] = acc[at]
        trade(r, k)

    work.run(finished)
    for r in range(1, 4):
        pltpu.make_async_copy(traded.at[r - 1], traded.at[r - 1], recv_sem.at[r - 1]).wait()
        for k in range(pairs):
            out[:, column(r, 2 * k + parity[r])] = strips[r - 1, k]
            turned = traded[r - 1, k].T
            kept = turned[:rows]
            for d in range(1, shares):
                kept = jnp.where(place == d, turned[d * rows:(d + 1) * rows], kept)
            out[:, column(r, 2 * k + 1 - parity[r])] = kept
    work.end()
    for copy in trades:
        copy.wait_send()


def far_reduce(acc, near, devices, cameras, width):
    wide, columns = acc.shape
    bits = devices.bit_length() - 1
    rows = wide // devices
    pairs = GROUP_TILES // 2
    return pl.pallas_call(
        functools.partial(far_reduce_kernel, bits, width),
        name="far_reduce",
        out_shape=jax.ShapeDtypeStruct((rows, cameras * wide), jnp.float32),
        in_specs=[ANY, VMEM],
        out_specs=VMEM,
        scratch_shapes=reduction_scratch(bits, rows, width, columns // width)
        + [
            pltpu.VMEM((3, pairs, rows, width), jnp.float32),
            pltpu.VMEM((3, pairs, width, width), jnp.float32),
            pltpu.SemaphoreType.DMA((3 * pairs * width // rows,)),
            pltpu.SemaphoreType.DMA((3,)),
        ],
        compiler_params=pltpu.CompilerParams(
            collective_id=2, has_side_effects=True, vmem_limit_bytes=VMEM_LIMIT
        ),
    )(acc.reshape((2,) * bits + (rows, columns)), near)


def on_device(counts, tiles, cam_jac, point_jac, point_inv):
    devices = lax.axis_size("cluster")
    cameras = lax.axis_size("camera")
    width = cam_jac.shape[2]
    tiles = tiles.T
    near, early, coupled = exchange(
        cam_jac, point_jac.transpose(0, 2, 1, 3), point_inv.transpose(1, 2, 0, 3)
    )
    near_acc, left = near_sum(counts, tiles, cam_jac, near, coupled)
    near_strip, late = near_reduce(near_acc, cam_jac, devices)
    far_acc = far_sum(counts, tiles, left, early, late)
    return far_reduce(far_acc, near_strip, devices, cameras, width)[None]


def solution(mesh):
    in_specs = (
        P(),
        P(),
        P("cluster", None, "camera"),
        P("cluster", None, None, "camera"),
        P("cluster", None, None, "camera"),
    )
    out_specs = P("camera", "cluster", None)
    return jax.shard_map(
        on_device,
        mesh=mesh, in_specs=in_specs, out_specs=out_specs, check_vma=False,
    )
```

```python
import functools
import itertools

import jax
import jax.numpy as jnp
from jax import lax
from jax.experimental import pallas as pl
from jax.experimental.pallas import tpu as pltpu
from jax.sharding import PartitionSpec as P

MESH = pl.DeviceIdType.MESH
ANY = pl.BlockSpec(memory_space=pl.ANY)
VMEM = pl.BlockSpec(memory_space=pltpu.VMEM)
SMEM = pl.BlockSpec(memory_space=pltpu.SMEM)
LANES = 128
GROUP_TILES = 4
STRIDE = 4
FAR_STRIDE = 2
CHUNKS = 2
VMEM_LIMIT = 56 * 1024 * 1024


def early_slots(slots):
    return 3 * slots // 8


def halves(x):
    high = x.astype(jnp.bfloat16)
    low = (x - high.astype(jnp.float32)).astype(jnp.bfloat16)
    return high, low


def dot3(left, right, dims):
    lh, ll = halves(left)
    rh, rl = halves(right)
    (ld,), (rd,) = dims
    return lax.dot_general(
        jnp.concatenate([lh, lh, ll], axis=ld),
        jnp.concatenate([rh, rl, rh], axis=rd),
        (dims, ((), ())),
        preferred_element_type=jnp.float32,
    )


def greet(peers):
    barrier = pltpu.get_barrier_semaphore()
    for peer in peers:
        pl.semaphore_signal(barrier, inc=1, device_id=peer, device_id_type=MESH)
    pl.semaphore_wait(barrier, len(peers))


def send(src, dst, send_sem, recv_sem, peer):
    return pltpu.make_async_remote_copy(
        src_ref=src, dst_ref=dst, send_sem=send_sem, recv_sem=recv_sem,
        device_id=peer, device_id_type=MESH,
    )


def exchange_kernel(
    jac, points, inv, near, far, coupled,
    points_here, outgoing, arrived, mine, packed, across_in,
    send_sem, recv_sem, local_sem,
):
    camera = lax.axis_index("camera")
    core = lax.rem(camera, 2)
    sibling = {"camera": camera + 1 - 2 * core}
    across = {"camera": lax.rem(camera + 2, 4)}
    half = coupled.shape[0] // 2
    quarter = half // 2
    own, theirs = core * half, (1 - core) * half
    starts = [theirs, own, theirs + quarter, own + quarter]

    loads = [
        pltpu.make_async_copy(
            points.at[pl.ds(start, quarter)], points_here.at[which], local_sem.at[which]
        )
        for which, start in enumerate(starts)
    ]
    for load in loads:
        load.start()
    greet([sibling, across])

    def copy_to(which, src, dst, peer):
        copy = send(src, dst, send_sem.at[which], recv_sem.at[which], peer)
        copy.start()
        return copy

    to_across = copy_to(0, jac.at[pl.ds(0, far.shape[1])], far.at[0], across)
    to_sibling = copy_to(1, jac, near, sibling)

    def couple(which, target):
        def body(i, carry):
            p = [points_here[which, i, j] for j in range(3)]
            w = [
                sum(p[j] * inv[j, k, pl.ds(starts[which] + i, 1), :] for j in range(3))
                for k in range(3)
            ]
            target[which // 2, i] = dot3(
                jnp.concatenate(w, axis=1), jnp.concatenate(p, axis=1), (((1,), (1,)))
            )
            return carry

        loads[which].wait()
        lax.fori_loop(0, quarter, body, 0, unroll=2)

    rows = coupled.shape[1]
    row = lax.broadcasted_iota(jnp.int32, (rows, rows), 0)
    col = lax.broadcasted_iota(jnp.int32, (rows, rows), 1)

    def pack(q):
        for i in range(quarter // 2):
            first, second = mine[q, 2 * i], mine[q, 2 * i + 1]
            diagonal = jnp.sum(jnp.where(row == col, second, 0.0), axis=0, keepdims=True)
            packed[q, i, :rows] = jnp.where(row <= col, first, second)
            packed[q, i, rows:] = jnp.broadcast_to(diagonal, (8, rows))

    def unpack(q, block):
        for i in range(quarter // 2):
            both = packed[q, i, :rows] + across_in[q, i, :rows]
            diagonal = packed[q, i, rows:rows + 1] + across_in[q, i, rows:rows + 1]
            turned = both.T
            block[2 * i] = jnp.where(row <= col, both, turned)
            block[2 * i + 1] = jnp.where(
                row == col, diagonal, jnp.where(row > col, both, turned)
            )

    sent, crossed, returned = [], [], []
    for q in range(2):
        couple(2 * q, outgoing)
        sent.append(copy_to(2 + q, outgoing.at[q], arrived.at[q], sibling))
        couple(2 * q + 1, mine)
        sent[q].wait_recv()
        mine[q] += arrived[q]
        pack(q)
        crossed.append(copy_to(4 + q, packed.at[q], across_in.at[q], across))
    to_across.wait_recv()
    forward = copy_to(6, far.at[0], far.at[1], sibling)
    for q in range(2):
        crossed[q].wait_recv()
        block = coupled.at[pl.ds(own + q * quarter, quarter)]
        unpack(q, block)
        returned.append(copy_to(7 + q, block, block, sibling))
    for copy in [to_across, to_sibling] + sent + crossed:
        copy.wait_send()
    to_sibling.wait_recv()
    forward.wait()
    for copy in returned:
        copy.wait()


def exchange(jac, points, inv):
    slots, rows, width = jac.shape
    quarter = slots // 4
    block = pltpu.VMEM((2, quarter, rows, rows), jnp.float32)
    triangles = pltpu.VMEM((2, quarter // 2, rows + 8, rows), jnp.float32)
    return pl.pallas_call(
        exchange_kernel,
        name="camera_exchange",
        out_shape=(
            jax.ShapeDtypeStruct((slots, rows, width), jnp.float32),
            jax.ShapeDtypeStruct((2, early_slots(slots), rows, width), jnp.float32),
            jax.ShapeDtypeStruct((slots, rows, rows), jnp.float32),
        ),
        in_specs=[ANY, ANY, VMEM],
        out_specs=(ANY, ANY, VMEM),
        scratch_shapes=[
            pltpu.VMEM((4, quarter) + points.shape[1:], jnp.float32),
            block, block, block, triangles, triangles,
            pltpu.SemaphoreType.DMA((9,)),
            pltpu.SemaphoreType.DMA((9,)),
            pltpu.SemaphoreType.DMA((4,)),
        ],
        compiler_params=pltpu.CompilerParams(
            collective_id=0, has_side_effects=True, vmem_limit_bytes=VMEM_LIMIT
        ),
    )(jac, points, inv)


def add_pair(tiles, acc, slot, camera, r, first, width, block):
    other = jnp.bitwise_xor(camera, r)
    row_tile, col_tile = tiles[camera, slot], tiles[other, slot]
    upper = (camera > other).astype(jnp.int32)

    @pl.when(lax.rem(row_tile + col_tile + upper, 2) == 0)
    def _():
        row = pl.ds(pl.multiple_of(row_tile * width, width), width)
        col = pl.multiple_of(first + (col_tile // 2) * width, width)
        acc[row, pl.ds(col, width)] += block


def near_kernel(counts, tiles, jac, near, coupled, acc, left):
    camera = lax.axis_index("camera")
    device = lax.axis_index("cluster")
    slots, _, width = jac.shape
    live = counts[device]
    acc[...] = jnp.zeros_like(acc)

    def one(c):
        panel = jac[c]
        schur = panel - dot3(coupled[c], panel, (((1,), (0,))))
        schur = schur * jnp.where(c < live, 1.0, 0.0)
        left[c] = schur
        return dot3(schur, jnp.concatenate([panel, near[c]], axis=1), (((0,), (0,))))

    def add(c, block):
        slot = device * slots + c
        row = pl.ds(pl.multiple_of(tiles[camera, slot] * width, width), width)
        acc[row, :width] += block[:, :width]
        add_pair(tiles, acc, slot, camera, 1, width, width, block[:, width:])

    def body(step, carry):
        blocks = [one(STRIDE * step + i) for i in range(STRIDE)]
        for i in range(STRIDE):
            add(STRIDE * step + i, blocks[i])
        return carry

    lax.fori_loop(0, (live + STRIDE - 1) // STRIDE, body, 0)


def near_sum(counts, tiles, jac, near, coupled):
    slots, rows, width = jac.shape
    return pl.pallas_call(
        near_kernel,
        name="near_sum",
        out_shape=(
            jax.ShapeDtypeStruct(
                (GROUP_TILES * width, (1 + GROUP_TILES // 2) * width), jnp.float32
            ),
            jax.ShapeDtypeStruct((slots, rows, width), jnp.float32),
        ),
        in_specs=[SMEM, SMEM, VMEM, VMEM, VMEM],
        out_specs=(VMEM, VMEM),
        compiler_params=pltpu.CompilerParams(vmem_limit_bytes=VMEM_LIMIT),
    )(counts, tiles, jac, near, coupled)


def far_kernel(counts, tiles, left, early, late, acc):
    camera = lax.axis_index("camera")
    device = lax.axis_index("cluster")
    slots, _, width = left.shape
    first = early.shape[1]
    live = counts[device]
    acc[...] = jnp.zeros_like(acc)

    def part(far, base, steps):
        def one(i):
            right = jnp.concatenate([far[0, i], far[1, i]], axis=1)
            return dot3(left[base + i], right, (((0,), (0,))))

        def add(i, block):
            slot = device * slots + base + i
            for r in (2, 3):
                cut = block[:, (r - 2) * width:(r - 1) * width]
                column = (r - 2) * (GROUP_TILES // 2) * width
                add_pair(tiles, acc, slot, camera, r, column, width, cut)

        def body(step, carry):
            blocks = [one(FAR_STRIDE * step + i) for i in range(FAR_STRIDE)]
            for i in range(FAR_STRIDE):
                add(FAR_STRIDE * step + i, blocks[i])
            return carry

        lax.fori_loop(0, steps, body, 0)

    steps = (live + FAR_STRIDE - 1) // FAR_STRIDE
    part(early, 0, jnp.minimum(steps, first // FAR_STRIDE))
    part(late, first, jnp.maximum(steps - first // FAR_STRIDE, 0))


def far_sum(counts, tiles, left, early, late):
    width = left.shape[2]
    return pl.pallas_call(
        far_kernel,
        name="far_sum",
        out_shape=jax.ShapeDtypeStruct(
            (GROUP_TILES * width, GROUP_TILES * width), jnp.float32
        ),
        in_specs=[SMEM, SMEM, VMEM, VMEM, VMEM],
        out_specs=VMEM,
        compiler_params=pltpu.CompilerParams(vmem_limit_bytes=VMEM_LIMIT),
    )(counts, tiles, left, early, late)


class Reduction:
    def __init__(self, bits, width, orders, given, acc, buffers, sems):
        self.bits, self.width, self.orders = bits, width, orders
        self.given, self.acc, self.buffers = given, acc, buffers
        self.send_sem, self.recv_sem, self.local_sem = sems
        device = lax.axis_index("cluster")
        self.bit = [lax.rem(device // (1 << b), 2) for b in range(bits)]
        self.peers = [
            {"cluster": device + (1 - 2 * self.bit[b]) * (1 << b)} for b in range(bits)
        ]
        self.copies = {}

    def load(self):
        self.loads = []
        for part in range(len(self.orders)):
            at = (slice(None),) * (self.bits + 1) + (self.columns(part),)
            copy = pltpu.make_async_copy(
                self.given.at[at], self.acc.at[at], self.local_sem.at[part]
            )
            copy.start()
            self.loads.append(copy)

    def columns(self, part):
        return pl.ds(part * self.width, self.width)

    def region(self, part, step, flip):
        index = [slice(None)] * self.bits
        order = self.orders[part]
        for b in order[:step]:
            index[self.bits - 1 - b] = self.bit[b]
        b = order[step]
        index[self.bits - 1 - b] = 1 - self.bit[b] if flip else self.bit[b]
        return index

    def start(self, part, step):
        which = part * self.bits + step
        source = self.acc if step else self.given
        index = tuple(self.region(part, step, True))
        copy = send(
            source.at[index + (slice(None), self.columns(part))], self.buffers[which],
            self.send_sem.at[which], self.recv_sem.at[which],
            self.peers[self.orders[part][step]],
        )
        copy.start()
        self.copies[part, step] = copy

    def begin(self):
        for part in range(len(self.orders)):
            self.start(part, 0)

    def run(self, finished, between=lambda step: None):
        for step in range(self.bits):
            for part in range(len(self.orders)):
                if step == 0:
                    self.loads[part].wait()
                self.copies[part, step].wait_recv()
                index = self.region(part, step, False)
                free = [i for i in range(self.bits) if isinstance(index[i], slice)]
                for place in itertools.product(range(2), repeat=len(free)):
                    full = list(index)
                    for i, value in zip(free, place):
                        full[i] = value
                    at = tuple(full) + (slice(None), self.columns(part))
                    self.acc[at] += self.buffers[part * self.bits + step][place]
                if step + 1 < self.bits:
                    self.start(part, step + 1)
                else:
                    finished(part, tuple(reversed(self.bit)) + (slice(None), self.columns(part)))
            between(step)

    def end(self):
        for copy in self.copies.values():
            copy.wait_send()


def reduction_scratch(bits, rows, width, parts):
    count = parts * bits
    return (
        [pltpu.VMEM((2,) * bits + (rows, parts * width), jnp.float32)]
        + [
            pltpu.VMEM((2,) * (bits - 1 - step) + (rows, width), jnp.float32)
            for _ in range(parts)
            for step in range(bits)
        ]
        + [pltpu.SemaphoreType.DMA((n,)) for n in (count, count, parts)]
    )


def orders_of(bits, parts):
    straight = tuple(range(bits))
    swapped = (1, 0) + straight[2:]
    far_first = (bits - 1,) + straight[:-1]
    if parts % 2:
        return [(straight, swapped, far_first)[part % 3] for part in range(parts)]
    return [(straight, swapped)[part % 2] for part in range(parts)]


def near_reduce_kernel(bits, width, given, jac, out, far, acc, *scratch):
    parts = out.shape[1] // width
    buffers, sems = scratch[:parts * bits], scratch[parts * bits:-2]
    send_sem, recv_sem = scratch[-2:]
    camera = lax.axis_index("camera")
    sibling = {"camera": camera + 1 - 2 * lax.rem(camera, 2)}
    across = {"camera": lax.rem(camera + 2, 4)}
    work = Reduction(bits, width, orders_of(bits, parts), given, acc, buffers, sems)
    work.load()
    greet(work.peers + [sibling, across])
    work.begin()
    late = far.shape[1]
    chunk = late // CHUNKS
    to_across, forwards = [], []
    for i in range(CHUNKS):
        to_across.append(send(
            jac.at[pl.ds(jac.shape[0] - late + i * chunk, chunk)],
            far.at[0, pl.ds(i * chunk, chunk)],
            send_sem.at[i], recv_sem.at[i], across,
        ))
        to_across[i].start()

    def forward(i):
        to_across[i].wait_recv()
        part = pl.ds(i * chunk, chunk)
        forwards.append(send(
            far.at[0, part], far.at[1, part],
            send_sem.at[CHUNKS + i], recv_sem.at[CHUNKS + i], sibling,
        ))
        forwards[i].start()

    def finished(part, at):
        out[:, part * width:(part + 1) * width] = acc[at]

    def between(step):
        if 1 <= step <= CHUNKS:
            forward(step - 1)

    work.run(finished, between)
    for i in range(len(forwards), CHUNKS):
        forward(i)
    work.end()
    for copy in to_across:
        copy.wait_send()
    for copy in forwards:
        copy.wait()


def near_reduce(acc, jac, devices):
    wide, columns = acc.shape
    slots, depth, width = jac.shape
    bits = devices.bit_length() - 1
    rows = wide // devices
    return pl.pallas_call(
        functools.partial(near_reduce_kernel, bits, width),
        name="near_reduce",
        out_shape=(
            jax.ShapeDtypeStruct((rows, columns), jnp.float32),
            jax.ShapeDtypeStruct((2, slots - early_slots(slots), depth, width), jnp.float32),
        ),
        in_specs=[ANY, ANY],
        out_specs=(VMEM, ANY),
        scratch_shapes=reduction_scratch(bits, rows, width, columns // width)
        + [pltpu.SemaphoreType.DMA((2 * CHUNKS,))] * 2,
        compiler_params=pltpu.CompilerParams(
            collective_id=1, has_side_effects=True, vmem_limit_bytes=VMEM_LIMIT
        ),
    )(acc.reshape((2,) * bits + (rows, columns)), jac)


def far_reduce_kernel(bits, width, given, near, out, acc, *scratch):
    parts = GROUP_TILES
    pairs = GROUP_TILES // 2
    buffers, sems = scratch[:parts * bits], scratch[parts * bits:-4]
    strips, traded, send_sem, recv_sem = scratch[-4:]
    camera = lax.axis_index("camera")
    device = lax.axis_index("cluster")
    rows = out.shape[0]
    shares = width // rows
    tile, place = device // shares, lax.rem(device, shares)
    work = Reduction(bits, width, orders_of(bits, parts), given, acc, buffers, sems)
    work.load()

    other = [jnp.bitwise_xor(camera, r) for r in range(4)]
    parity = [lax.rem(tile + (camera > other[r]).astype(jnp.int32), 2) for r in range(4)]
    barrier = pltpu.get_barrier_semaphore()
    for peer in work.peers:
        pl.semaphore_signal(barrier, inc=1, device_id=peer, device_id_type=MESH)
    for r in range(1, 4):
        for k in range(pairs):
            for d in range(shares):
                peer = {
                    "camera": other[r], "cluster": (2 * k + 1 - parity[r]) * shares + d
                }
                pl.semaphore_signal(barrier, inc=1, device_id=peer, device_id_type=MESH)
    pl.semaphore_wait(barrier, bits + 3 * pairs * shares)

    trades = []

    def trade(r, k):
        for d in range(shares):
            copy = send(
                strips.at[r - 1, k],
                traded.at[r - 1, tile // 2, pl.ds(place * rows, rows)],
                send_sem.at[((r - 1) * pairs + k) * shares + d], recv_sem.at[r - 1],
                {"camera": other[r], "cluster": (2 * k + parity[r]) * shares + d},
            )
            copy.start()
            trades.append(copy)

    def column(r, t):
        return pl.ds(pl.multiple_of((other[r] * GROUP_TILES + t) * width, width), width)

    work.begin()
    for k in range(pairs):
        strips[0, k] = near[:, (1 + k) * width:(2 + k) * width]
        trade(1, k)
    for t in range(GROUP_TILES):
        out[:, column(0, t)] = jnp.where(t == tile, near[:, :width], 0.0)

    def finished(part, at):
        r, k = 2 + part // pairs, part % pairs
        strips[r - 1, k] = acc[at]
        trade(r, k)

    work.run(finished)
    for r in range(1, 4):
        pltpu.make_async_copy(traded.at[r - 1], traded.at[r - 1], recv_sem.at[r - 1]).wait()
        for k in range(pairs):
            out[:, column(r, 2 * k + parity[r])] = strips[r - 1, k]
            turned = traded[r - 1, k].T
            kept = turned[:rows]
            for d in range(1, shares):
                kept = jnp.where(place == d, turned[d * rows:(d + 1) * rows], kept)
            out[:, column(r, 2 * k + 1 - parity[r])] = kept
    work.end()
    for copy in trades:
        copy.wait_send()


def far_reduce(acc, near, devices, cameras, width):
    wide, columns = acc.shape
    bits = devices.bit_length() - 1
    rows = wide // devices
    pairs = GROUP_TILES // 2
    return pl.pallas_call(
        functools.partial(far_reduce_kernel, bits, width),
        name="far_reduce",
        out_shape=jax.ShapeDtypeStruct((rows, cameras * wide), jnp.float32),
        in_specs=[ANY, VMEM],
        out_specs=VMEM,
        scratch_shapes=reduction_scratch(bits, rows, width, columns // width)
        + [
            pltpu.VMEM((3, pairs, rows, width), jnp.float32),
            pltpu.VMEM((3, pairs, width, width), jnp.float32),
            pltpu.SemaphoreType.DMA((3 * pairs * width // rows,)),
            pltpu.SemaphoreType.DMA((3,)),
        ],
        compiler_params=pltpu.CompilerParams(
            collective_id=2, has_side_effects=True, vmem_limit_bytes=VMEM_LIMIT
        ),
    )(acc.reshape((2,) * bits + (rows, columns)), near)


def on_device(counts, tiles, cam_jac, point_jac, point_inv):
    devices = lax.axis_size("cluster")
    cameras = lax.axis_size("camera")
    width = cam_jac.shape[2]
    tiles = tiles.T
    near, early, coupled = exchange(
        cam_jac, point_jac.transpose(0, 2, 1, 3), point_inv.transpose(1, 2, 0, 3)
    )
    near_acc, left = near_sum(counts, tiles, cam_jac, near, coupled)
    near_strip, late = near_reduce(near_acc, cam_jac, devices)
    far_acc = far_sum(counts, tiles, left, early, late)
    return far_reduce(far_acc, near_strip, devices, cameras, width)[None]


def solution(mesh):
    in_specs = (
        P(),
        P(),
        P("cluster", None, "camera"),
        P("cluster", None, None, "camera"),
        P("cluster", None, None, "camera"),
    )
    out_specs = P("camera", "cluster", None)
    return jax.shard_map(
        on_device,
        mesh=mesh, in_specs=in_specs, out_specs=out_specs, check_vma=False,
    )
```

```python
import functools
import itertools

import jax
import jax.numpy as jnp
from jax import lax
from jax.experimental import pallas as pl
from jax.experimental.pallas import tpu as pltpu
from jax.sharding import PartitionSpec as P

MESH = pl.DeviceIdType.MESH
ANY = pl.BlockSpec(memory_space=pl.ANY)
VMEM = pl.BlockSpec(memory_space=pltpu.VMEM)
SMEM = pl.BlockSpec(memory_space=pltpu.SMEM)
LANES = 128
GROUP_TILES = 4
STRIDE = 4
FAR_STRIDE = 2
CHUNKS = 2
VMEM_LIMIT = 56 * 1024 * 1024


def early_slots(slots):
    return 3 * slots // 8


def halves(x):
    high = x.astype(jnp.bfloat16)
    low = (x - high.astype(jnp.float32)).astype(jnp.bfloat16)
    return high, low


def dot3(left, right, dims):
    lh, ll = halves(left)
    rh, rl = halves(right)
    (ld,), (rd,) = dims
    return lax.dot_general(
        jnp.concatenate([lh, lh, ll], axis=ld),
        jnp.concatenate([rh, rl, rh], axis=rd),
        (dims, ((), ())),
        preferred_element_type=jnp.float32,
    )


def greet(peers):
    barrier = pltpu.get_barrier_semaphore()
    for peer in peers:
        pl.semaphore_signal(barrier, inc=1, device_id=peer, device_id_type=MESH)
    pl.semaphore_wait(barrier, len(peers))


def send(src, dst, send_sem, recv_sem, peer):
    return pltpu.make_async_remote_copy(
        src_ref=src, dst_ref=dst, send_sem=send_sem, recv_sem=recv_sem,
        device_id=peer, device_id_type=MESH,
    )


def exchange_kernel(
    jac, points, inv, near, far, coupled,
    points_here, outgoing, arrived, mine, packed, across_in,
    send_sem, recv_sem, local_sem,
):
    camera = lax.axis_index("camera")
    core = lax.rem(camera, 2)
    sibling = {"camera": camera + 1 - 2 * core}
    across = {"camera": lax.rem(camera + 2, 4)}
    half = coupled.shape[0] // 2
    quarter = half // 2
    own, theirs = core * half, (1 - core) * half
    starts = [theirs, own, theirs + quarter, own + quarter]

    loads = [
        pltpu.make_async_copy(
            points.at[pl.ds(start, quarter)], points_here.at[which], local_sem.at[which]
        )
        for which, start in enumerate(starts)
    ]
    for load in loads:
        load.start()
    greet([sibling, across])

    def copy_to(which, src, dst, peer):
        copy = send(src, dst, send_sem.at[which], recv_sem.at[which], peer)
        copy.start()
        return copy

    to_across = copy_to(0, jac.at[pl.ds(0, far.shape[1])], far.at[0], across)
    to_sibling = copy_to(1, jac, near, sibling)

    def couple(which, target):
        def body(i, carry):
            p = [points_here[which, i, j] for j in range(3)]
            w = [
                sum(p[j] * inv[j, k, pl.ds(starts[which] + i, 1), :] for j in range(3))
                for k in range(3)
            ]
            target[which // 2, i] = dot3(
                jnp.concatenate(w, axis=1), jnp.concatenate(p, axis=1), (((1,), (1,)))
            )
            return carry

        loads[which].wait()
        lax.fori_loop(0, quarter, body, 0, unroll=2)

    rows = coupled.shape[1]
    row = lax.broadcasted_iota(jnp.int32, (rows, rows), 0)
    col = lax.broadcasted_iota(jnp.int32, (rows, rows), 1)

    def pack(q):
        for i in range(quarter // 2):
            first, second = mine[q, 2 * i], mine[q, 2 * i + 1]
            diagonal = jnp.sum(jnp.where(row == col, second, 0.0), axis=0, keepdims=True)
            packed[q, i, :rows] = jnp.where(row <= col, first, second)
            packed[q, i, rows:] = jnp.broadcast_to(diagonal, (8, rows))

    def unpack(q, block):
        for i in range(quarter // 2):
            both = packed[q, i, :rows] + across_in[q, i, :rows]
            diagonal = packed[q, i, rows:rows + 1] + across_in[q, i, rows:rows + 1]
            turned = both.T
            block[2 * i] = jnp.where(row <= col, both, turned)
            block[2 * i + 1] = jnp.where(
                row == col, diagonal, jnp.where(row > col, both, turned)
            )

    sent, crossed, returned = [], [], []
    for q in range(2):
        couple(2 * q, outgoing)
        sent.append(copy_to(2 + q, outgoing.at[q], arrived.at[q], sibling))
        couple(2 * q + 1, mine)
        sent[q].wait_recv()
        mine[q] += arrived[q]
        pack(q)
        crossed.append(copy_to(4 + q, packed.at[q], across_in.at[q], across))
    to_across.wait_recv()
    forward = copy_to(6, far.at[0], far.at[1], sibling)
    for q in range(2):
        crossed[q].wait_recv()
        block = coupled.at[pl.ds(own + q * quarter, quarter)]
        unpack(q, block)
        returned.append(copy_to(7 + q, block, block, sibling))
    for copy in [to_across, to_sibling] + sent + crossed:
        copy.wait_send()
    to_sibling.wait_recv()
    forward.wait()
    for copy in returned:
        copy.wait()


def exchange(jac, points, inv):
    slots, rows, width = jac.shape
    quarter = slots // 4
    block = pltpu.VMEM((2, quarter, rows, rows), jnp.float32)
    triangles = pltpu.VMEM((2, quarter // 2, rows + 8, rows), jnp.float32)
    return pl.pallas_call(
        exchange_kernel,
        name="camera_exchange",
        out_shape=(
            jax.ShapeDtypeStruct((slots, rows, width), jnp.float32),
            jax.ShapeDtypeStruct((2, early_slots(slots), rows, width), jnp.float32),
            jax.ShapeDtypeStruct((slots, rows, rows), jnp.float32),
        ),
        in_specs=[ANY, ANY, VMEM],
        out_specs=(ANY, ANY, VMEM),
        scratch_shapes=[
            pltpu.VMEM((4, quarter) + points.shape[1:], jnp.float32),
            block, block, block, triangles, triangles,
            pltpu.SemaphoreType.DMA((9,)),
            pltpu.SemaphoreType.DMA((9,)),
            pltpu.SemaphoreType.DMA((4,)),
        ],
        compiler_params=pltpu.CompilerParams(
            collective_id=0, has_side_effects=True, vmem_limit_bytes=VMEM_LIMIT
        ),
    )(jac, points, inv)


def add_pair(tiles, acc, slot, camera, r, first, width, block):
    other = jnp.bitwise_xor(camera, r)
    row_tile, col_tile = tiles[camera, slot], tiles[other, slot]
    upper = (camera > other).astype(jnp.int32)

    @pl.when(lax.rem(row_tile + col_tile + upper, 2) == 0)
    def _():
        row = pl.ds(pl.multiple_of(row_tile * width, width), width)
        col = pl.multiple_of(first + (col_tile // 2) * width, width)
        acc[row, pl.ds(col, width)] += block


def near_kernel(counts, tiles, jac, near, coupled, acc, left):
    camera = lax.axis_index("camera")
    device = lax.axis_index("cluster")
    slots, _, width = jac.shape
    live = counts[device]
    acc[...] = jnp.zeros_like(acc)

    def one(c):
        panel = jac[c]
        schur = panel - dot3(coupled[c], panel, (((1,), (0,))))
        schur = schur * jnp.where(c < live, 1.0, 0.0)
        left[c] = schur
        return dot3(schur, jnp.concatenate([panel, near[c]], axis=1), (((0,), (0,))))

    def add(c, block):
        slot = device * slots + c
        row = pl.ds(pl.multiple_of(tiles[camera, slot] * width, width), width)
        acc[row, :width] += block[:, :width]
        add_pair(tiles, acc, slot, camera, 1, width, width, block[:, width:])

    def body(step, carry):
        blocks = [one(STRIDE * step + i) for i in range(STRIDE)]
        for i in range(STRIDE):
            add(STRIDE * step + i, blocks[i])
        return carry

    lax.fori_loop(0, (live + STRIDE - 1) // STRIDE, body, 0)


def near_sum(counts, tiles, jac, near, coupled):
    slots, rows, width = jac.shape
    return pl.pallas_call(
        near_kernel,
        name="near_sum",
        out_shape=(
            jax.ShapeDtypeStruct(
                (GROUP_TILES * width, (1 + GROUP_TILES // 2) * width), jnp.float32
            ),
            jax.ShapeDtypeStruct((slots, rows, width), jnp.float32),
        ),
        in_specs=[SMEM, SMEM, VMEM, VMEM, VMEM],
        out_specs=(VMEM, VMEM),
        compiler_params=pltpu.CompilerParams(vmem_limit_bytes=VMEM_LIMIT),
    )(counts, tiles, jac, near, coupled)


def far_kernel(counts, tiles, left, early, late, acc):
    camera = lax.axis_index("camera")
    device = lax.axis_index("cluster")
    slots, _, width = left.shape
    first = early.shape[1]
    live = counts[device]
    acc[...] = jnp.zeros_like(acc)

    def part(far, base, steps):
        def one(i):
            right = jnp.concatenate([far[0, i], far[1, i]], axis=1)
            return dot3(left[base + i], right, (((0,), (0,))))

        def add(i, block):
            slot = device * slots + base + i
            for r in (2, 3):
                cut = block[:, (r - 2) * width:(r - 1) * width]
                column = (r - 2) * (GROUP_TILES // 2) * width
                add_pair(tiles, acc, slot, camera, r, column, width, cut)

        def body(step, carry):
            blocks = [one(FAR_STRIDE * step + i) for i in range(FAR_STRIDE)]
            for i in range(FAR_STRIDE):
                add(FAR_STRIDE * step + i, blocks[i])
            return carry

        lax.fori_loop(0, steps, body, 0)

    steps = (live + FAR_STRIDE - 1) // FAR_STRIDE
    part(early, 0, jnp.minimum(steps, first // FAR_STRIDE))
    part(late, first, jnp.maximum(steps - first // FAR_STRIDE, 0))


def far_sum(counts, tiles, left, early, late):
    width = left.shape[2]
    return pl.pallas_call(
        far_kernel,
        name="far_sum",
        out_shape=jax.ShapeDtypeStruct(
            (GROUP_TILES * width, GROUP_TILES * width), jnp.float32
        ),
        in_specs=[SMEM, SMEM, VMEM, VMEM, VMEM],
        out_specs=VMEM,
        compiler_params=pltpu.CompilerParams(vmem_limit_bytes=VMEM_LIMIT),
    )(counts, tiles, left, early, late)


class Reduction:
    def __init__(self, bits, width, orders, given, acc, buffers, sems):
        self.bits, self.width, self.orders = bits, width, orders
        self.given, self.acc, self.buffers = given, acc, buffers
        self.send_sem, self.recv_sem, self.local_sem = sems
        device = lax.axis_index("cluster")
        self.bit = [lax.rem(device // (1 << b), 2) for b in range(bits)]
        self.peers = [
            {"cluster": device + (1 - 2 * self.bit[b]) * (1 << b)} for b in range(bits)
        ]
        self.copies = {}

    def load(self):
        self.loads = []
        for part in range(len(self.orders)):
            at = (slice(None),) * (self.bits + 1) + (self.columns(part),)
            copy = pltpu.make_async_copy(
                self.given.at[at], self.acc.at[at], self.local_sem.at[part]
            )
            copy.start()
            self.loads.append(copy)

    def columns(self, part):
        return pl.ds(part * self.width, self.width)

    def region(self, part, step, flip):
        index = [slice(None)] * self.bits
        order = self.orders[part]
        for b in order[:step]:
            index[self.bits - 1 - b] = self.bit[b]
        b = order[step]
        index[self.bits - 1 - b] = 1 - self.bit[b] if flip else self.bit[b]
        return index

    def start(self, part, step):
        which = part * self.bits + step
        source = self.acc if step else self.given
        index = tuple(self.region(part, step, True))
        copy = send(
            source.at[index + (slice(None), self.columns(part))], self.buffers[which],
            self.send_sem.at[which], self.recv_sem.at[which],
            self.peers[self.orders[part][step]],
        )
        copy.start()
        self.copies[part, step] = copy

    def begin(self):
        for part in range(len(self.orders)):
            self.start(part, 0)

    def run(self, finished, between=lambda step: None):
        for step in range(self.bits):
            for part in range(len(self.orders)):
                if step == 0:
                    self.loads[part].wait()
                self.copies[part, step].wait_recv()
                index = self.region(part, step, False)
                free = [i for i in range(self.bits) if isinstance(index[i], slice)]
                for place in itertools.product(range(2), repeat=len(free)):
                    full = list(index)
                    for i, value in zip(free, place):
                        full[i] = value
                    at = tuple(full) + (slice(None), self.columns(part))
                    self.acc[at] += self.buffers[part * self.bits + step][place]
                if step + 1 < self.bits:
                    self.start(part, step + 1)
                else:
                    finished(part, tuple(reversed(self.bit)) + (slice(None), self.columns(part)))
            between(step)

    def end(self):
        for copy in self.copies.values():
            copy.wait_send()


def reduction_scratch(bits, rows, width, parts):
    count = parts * bits
    return (
        [pltpu.VMEM((2,) * bits + (rows, parts * width), jnp.float32)]
        + [
            pltpu.VMEM((2,) * (bits - 1 - step) + (rows, width), jnp.float32)
            for _ in range(parts)
            for step in range(bits)
        ]
        + [pltpu.SemaphoreType.DMA((n,)) for n in (count, count, parts)]
    )


def orders_of(bits, parts):
    straight = tuple(range(bits))
    swapped = (1, 0) + straight[2:]
    far_first = (bits - 1,) + straight[:-1]
    return [(straight, swapped, far_first)[part % 3] for part in range(parts)]


def near_reduce_kernel(bits, width, given, jac, out, far, acc, *scratch):
    parts = out.shape[1] // width
    buffers, sems = scratch[:parts * bits], scratch[parts * bits:-2]
    send_sem, recv_sem = scratch[-2:]
    camera = lax.axis_index("camera")
    sibling = {"camera": camera + 1 - 2 * lax.rem(camera, 2)}
    across = {"camera": lax.rem(camera + 2, 4)}
    work = Reduction(bits, width, orders_of(bits, parts), given, acc, buffers, sems)
    work.load()
    greet(work.peers + [sibling, across])
    work.begin()
    late = far.shape[1]
    chunk = late // CHUNKS
    to_across, forwards = [], []
    for i in range(CHUNKS):
        to_across.append(send(
            jac.at[pl.ds(jac.shape[0] - late + i * chunk, chunk)],
            far.at[0, pl.ds(i * chunk, chunk)],
            send_sem.at[i], recv_sem.at[i], across,
        ))
        to_across[i].start()

    def forward(i):
        to_across[i].wait_recv()
        part = pl.ds(i * chunk, chunk)
        forwards.append(send(
            far.at[0, part], far.at[1, part],
            send_sem.at[CHUNKS + i], recv_sem.at[CHUNKS + i], sibling,
        ))
        forwards[i].start()

    def finished(part, at):
        out[:, part * width:(part + 1) * width] = acc[at]

    def between(step):
        if 1 <= step <= CHUNKS:
            forward(step - 1)

    work.run(finished, between)
    for i in range(len(forwards), CHUNKS):
        forward(i)
    work.end()
    for copy in to_across:
        copy.wait_send()
    for copy in forwards:
        copy.wait()


def near_reduce(acc, jac, devices):
    wide, columns = acc.shape
    slots, depth, width = jac.shape
    bits = devices.bit_length() - 1
    rows = wide // devices
    return pl.pallas_call(
        functools.partial(near_reduce_kernel, bits, width),
        name="near_reduce",
        out_shape=(
            jax.ShapeDtypeStruct((rows, columns), jnp.float32),
            jax.ShapeDtypeStruct((2, slots - early_slots(slots), depth, width), jnp.float32),
        ),
        in_specs=[ANY, ANY],
        out_specs=(VMEM, ANY),
        scratch_shapes=reduction_scratch(bits, rows, width, columns // width)
        + [pltpu.SemaphoreType.DMA((2 * CHUNKS,))] * 2,
        compiler_params=pltpu.CompilerParams(
            collective_id=1, has_side_effects=True, vmem_limit_bytes=VMEM_LIMIT
        ),
    )(acc.reshape((2,) * bits + (rows, columns)), jac)


def far_reduce_kernel(bits, width, given, near, out, acc, *scratch):
    parts = GROUP_TILES
    pairs = GROUP_TILES // 2
    buffers, sems = scratch[:parts * bits], scratch[parts * bits:-4]
    strips, traded, send_sem, recv_sem = scratch[-4:]
    camera = lax.axis_index("camera")
    device = lax.axis_index("cluster")
    rows = out.shape[0]
    shares = width // rows
    tile, place = device // shares, lax.rem(device, shares)
    work = Reduction(bits, width, orders_of(bits, parts), given, acc, buffers, sems)
    work.load()

    other = [jnp.bitwise_xor(camera, r) for r in range(4)]
    parity = [lax.rem(tile + (camera > other[r]).astype(jnp.int32), 2) for r in range(4)]
    barrier = pltpu.get_barrier_semaphore()
    for peer in work.peers:
        pl.semaphore_signal(barrier, inc=1, device_id=peer, device_id_type=MESH)
    for r in range(1, 4):
        for k in range(pairs):
            for d in range(shares):
                peer = {
                    "camera": other[r], "cluster": (2 * k + 1 - parity[r]) * shares + d
                }
                pl.semaphore_signal(barrier, inc=1, device_id=peer, device_id_type=MESH)
    pl.semaphore_wait(barrier, bits + 3 * pairs * shares)

    trades = []

    def trade(r, k):
        for d in range(shares):
            copy = send(
                strips.at[r - 1, k],
                traded.at[r - 1, tile // 2, pl.ds(place * rows, rows)],
                send_sem.at[((r - 1) * pairs + k) * shares + d], recv_sem.at[r - 1],
                {"camera": other[r], "cluster": (2 * k + parity[r]) * shares + d},
            )
            copy.start()
            trades.append(copy)

    def column(r, t):
        return pl.ds(pl.multiple_of((other[r] * GROUP_TILES + t) * width, width), width)

    work.begin()
    for k in range(pairs):
        strips[0, k] = near[:, (1 + k) * width:(2 + k) * width]
        trade(1, k)
    for t in range(GROUP_TILES):
        out[:, column(0, t)] = jnp.where(t == tile, near[:, :width], 0.0)

    def finished(part, at):
        r, k = 2 + part // pairs, part % pairs
        strips[r - 1, k] = acc[at]
        trade(r, k)

    work.run(finished)
    for r in range(1, 4):
        pltpu.make_async_copy(traded.at[r - 1], traded.at[r - 1], recv_sem.at[r - 1]).wait()
        for k in range(pairs):
            out[:, column(r, 2 * k + parity[r])] = strips[r - 1, k]
            turned = traded[r - 1, k].T
            kept = turned[:rows]
            for d in range(1, shares):
                kept = jnp.where(place == d, turned[d * rows:(d + 1) * rows], kept)
            out[:, column(r, 2 * k + 1 - parity[r])] = kept
    work.end()
    for copy in trades:
        copy.wait_send()


def far_reduce(acc, near, devices, cameras, width):
    wide, columns = acc.shape
    bits = devices.bit_length() - 1
    rows = wide // devices
    pairs = GROUP_TILES // 2
    return pl.pallas_call(
        functools.partial(far_reduce_kernel, bits, width),
        name="far_reduce",
        out_shape=jax.ShapeDtypeStruct((rows, cameras * wide), jnp.float32),
        in_specs=[ANY, VMEM],
        out_specs=VMEM,
        scratch_shapes=reduction_scratch(bits, rows, width, columns // width)
        + [
            pltpu.VMEM((3, pairs, rows, width), jnp.float32),
            pltpu.VMEM((3, pairs, width, width), jnp.float32),
            pltpu.SemaphoreType.DMA((3 * pairs * width // rows,)),
            pltpu.SemaphoreType.DMA((3,)),
        ],
        compiler_params=pltpu.CompilerParams(
            collective_id=2, has_side_effects=True, vmem_limit_bytes=VMEM_LIMIT
        ),
    )(acc.reshape((2,) * bits + (rows, columns)), near)


def on_device(counts, tiles, cam_jac, point_jac, point_inv):
    devices = lax.axis_size("cluster")
    cameras = lax.axis_size("camera")
    width = cam_jac.shape[2]
    tiles = tiles.T
    near, early, coupled = exchange(
        cam_jac, point_jac.transpose(0, 2, 1, 3), point_inv.transpose(1, 2, 0, 3)
    )
    near_acc, left = near_sum(counts, tiles, cam_jac, near, coupled)
    near_strip, late = near_reduce(near_acc, cam_jac, devices)
    far_acc = far_sum(counts, tiles, left, early, late)
    return far_reduce(far_acc, near_strip, devices, cameras, width)[None]


def solution(mesh):
    in_specs = (
        P(),
        P(),
        P("cluster", None, "camera"),
        P("cluster", None, None, "camera"),
        P("cluster", None, None, "camera"),
    )
    out_specs = P("camera", "cluster", None)
    return jax.shard_map(
        on_device,
        mesh=mesh, in_specs=in_specs, out_specs=out_specs, check_vma=False,
    )
```
